768 devices in a mesh: dp: 12 (over z), pool: 64 (over y, x, core).
Axes of the slice: x: 4, y: 8, z: 12, core: 2. Of those that a mesh axis runs over, the one named last changes fastest.
Arguments:
- queries: bfloat16 [1572864, 128], P(('dp', 'pool')), may hold values from -6 to 6
- cotangent: bfloat16 [1572864, 128], P(('dp', 'pool')), may hold values from -6 to 6
- owner: int32 [24576, 1], P(('dp', 'pool')), may hold values from 0 to 63; in each aligned block of 32 rows (0 to 31, 32 to 63, ...) at most 2 rows name the same one
- row: int32 [24576], P(('dp', 'pool')), may hold values from 0 to 7
- table: bfloat16 [6144, 256, 256], P(('dp', 'pool')), may hold values from -6 to 6
- lengths: int32 [6144, 2], P(('dp', 'pool')), may hold values from 16 to 128
- bias: float32 [1, 256], replicated, may hold values from -4 to 4
Outputs:
- attended: bfloat16 [1572864, 128], P(('dp', 'pool'))
- query_gradient: bfloat16 [1572864, 128], P(('dp', 'pool'))
- table_grad: bfloat16 [6144, 256, 256], P(('dp', 'pool'))
- bias_grad: float32 [1, 256], replicated
The draws below stay inside these ranges and needn't reach their ends.
Inputs may be any that keep to these rules, and one draw needn't show every extreme that they name: Among the spans of one device at most 2 name the same owner; some owner is named by exactly 2 of them on some devices.
All inputs are finite; a program needn't handle non-finite values.
Results may differ from the reference program's by a relative error of at most 0.0067.
Values may be sent and summed in bfloat16 or wider, within the bound.
A program may use at most 128 MiB of HBM per device.

```python
import math
import jax
import jax.numpy as jnp
import numpy as np
from jax import lax

HD = 128
HEADS = 1
SPAN = 64
NEIGH = 2
NBR_LEN = 128
CH_DEV = 32
NB_DEV = 8
CAP = 2
KEYS = 256
SPANS = 24576
TOKENS = 1572864
SETS = 6144
N_DP = 12
N_POOL = 64


def set_ends(entries, stream_key, smallest, high):
    index_at = [jax.random.randint(jax.random.fold_in(stream_key, axis), (), 0, length) for axis, length in enumerate(entries.shape)]
    main_axis = entries.shape.index(max(entries.shape))
    neighbour = index_at[:main_axis] + [(index_at[main_axis] + 1) % entries.shape[main_axis]] + index_at[main_axis + 1:]
    return entries.at[tuple(index_at)].set(smallest).at[tuple(neighbour)].set(high)


def levels(stream_key, extent, shards, low, top_value):
    def one(dim, blocks):
        steps = jax.random.uniform(jax.random.fold_in(jax.random.fold_in(stream_key, 6), dim), (blocks,), jnp.float32, low / len(shards), top_value / len(shards))
        return jnp.repeat(jnp.exp(steps), extent[dim] // blocks).reshape((-1,) + (1,) * (len(extent) - dim - 1))

    gain = one(*shards[0])
    for cut in shards[1:]:
        gain = gain * one(*cut)
    return gain


def shared_out(rng, own, number, rows, number_of, top, reach, slope):
    ranking = jax.random.permutation(rng, number_of)
    heavy_load, usual = portions_of(number_of, rows * top, reach, slope, True), portions_of(number_of, rows * top, reach, slope, False)
    places = jnp.arange(number_of)

    def named(sizes, offset_by):
        used = int((sizes > 0).sum())
        fixed = max(1, used // 4)
        passed = fixed + (places - fixed + offset_by * (used - fixed)) % max(1, number_of - fixed)
        return jnp.zeros((number_of,), jnp.int32).at[ranking[jnp.where(places < fixed, places, passed)]].set(jnp.asarray(sizes, jnp.int32))

    sizes = jnp.where(number % 4 == 0, named(heavy_load, number // 4), named(usual, number - number // 4 - 1))
    mixed = jax.random.permutation(jax.random.fold_in(own, 3), number_of)
    source_of, sink = mixed[0:number_of // 2 * 2:2], mixed[1:number_of // 2 * 2:2]
    slack = jnp.minimum(sizes[source_of] - 1, reach - sizes[sink]) // 2
    slack = jnp.where((source_of == ranking[0]) | (sink == ranking[0]) | (sizes[sink] == 0), 0, jnp.maximum(slack, 0))
    passed = jax.random.randint(jax.random.fold_in(own, 4), (number_of // 2,), 0, 1 << 20) % (slack + 1)
    sizes = sizes.at[source_of].add(-passed).at[sink].add(passed)
    labels = jnp.searchsorted(jnp.cumsum(sizes), jnp.arange(rows * top), side="right").astype(jnp.int32)
    listing = labels.reshape(top, rows).T
    listing = listing[jax.random.permutation(jax.random.fold_in(own, 1), rows)]
    offset_by = jax.random.randint(jax.random.fold_in(own, 2), (rows, 1), 0, top)
    return jnp.take_along_axis(listing, (jnp.arange(top)[None, :] + offset_by) % top, axis=1)


def portions_of(amount, total, bound, skew, full):
    weights = [(1 << 20) // math.isqrt(grade ** skew) + 1 for grade in range(1, amount + 1)]
    largest = bound if full else min(bound, max(-(-total // amount), total * weights[0] // sum(weights)))
    least = 1 if total - largest >= amount - 1 else 0
    holding, spare = [largest] + [least] * (amount - 1), total - largest - least * (amount - 1)
    while spare > 0:
        candidates = [i for i in range(1, amount) if holding[i] < largest] or [i for i in range(1, amount) if holding[i] < bound]
        mass, remaining = sum([weights[i] for i in candidates]), spare
        for i in candidates:
            addition = min(bound - holding[i], max(1, remaining * weights[i] // mass), spare)
            holding[i] = holding[i] + addition
            spare = spare - addition
    return np.array(holding)


def bell_draw(rng, dims, scale, most, cuts=(), kind=jnp.bfloat16):
    drawn = jax.random.normal(rng, dims, jnp.float32) * scale
    if len(cuts) > 0:
        drawn = levels(rng, dims, cuts, -0.22, 0.18) * drawn
    return jnp.clip(drawn, min=-most, max=most).astype(kind)


def setup_inputs(seed: int = 0) -> dict:
    splits = jax.random.split(jax.random.key(seed), 8)
    queries = bell_draw(splits[0], (TOKENS, HEADS * HD), 1.0, 6.0, ((0, 768),))
    cotangent = bell_draw(splits[1], (TOKENS, HEADS * HD), 1.0, 6.0, ((0, 768),))
    owner_keys = jax.random.split(jax.random.fold_in(splits[2], 1), SPANS // CH_DEV)
    owner_turns = jax.random.permutation(jax.random.fold_in(splits[2], 3), SPANS // CH_DEV)
    owner = jax.vmap(lambda own, number: shared_out(jax.random.fold_in(splits[2], 2), own, number, CH_DEV, N_POOL, 1, CAP, 2))(owner_keys, owner_turns).reshape((SPANS, 1))
    row = set_ends(jax.random.randint(splits[3], (SPANS,), 0, NB_DEV), jax.random.fold_in(splits[3], 1), 0, NB_DEV - 1).astype(jnp.int32)
    table = bell_draw(splits[4], (SETS, KEYS, 2 * HD), 1.0, 6.0, ((0, 768),))
    lengths = set_ends(jax.random.randint(splits[5], (SETS, NEIGH), max(1, NBR_LEN // 8), NBR_LEN + 1), jax.random.fold_in(splits[5], 1), max(1, NBR_LEN // 8), NBR_LEN).astype(jnp.int32)
    bias = bell_draw(splits[6], (HEADS, KEYS), 1.0, 4.0, (), jnp.float32)
    return dict(queries=queries, cotangent=cotangent, owner=owner, row=row, table=table, lengths=lengths, bias=bias)


def span_pass(query_block, incoming_cotangent_block, kv_blk, len_blk, row_bias_values):
    score_scale = HD ** -0.5
    neighbour_keys = kv_blk[:, :, :HD]
    neighbour_values = kv_blk[:, :, HD:]
    position = jnp.arange(NEIGH * NBR_LEN, dtype=jnp.int32)
    limit = jnp.repeat(len_blk, NBR_LEN, axis=1)
    live = (position % NBR_LEN)[None, :] < limit
    attention_scores = jnp.einsum('rft,rwt->rfw', query_block.astype(jnp.float32), neighbour_keys.astype(jnp.float32)) * score_scale + row_bias_values[None, None, :]
    attention_scores = jnp.where(live[:, None, :], attention_scores, -1e30)
    peak = jnp.max(attention_scores, axis=-1, keepdims=True)
    lse = peak + jnp.log(jnp.sum(jnp.exp(attention_scores - peak), axis=-1, keepdims=True))
    probs = jnp.exp(attention_scores - lse)
    attention_weights = probs.astype(jnp.bfloat16)
    attended = jnp.einsum('xtl,xls->xts', attention_weights.astype(jnp.float32), neighbour_values.astype(jnp.float32)).astype(jnp.bfloat16)
    delta = jnp.sum(incoming_cotangent_block.astype(jnp.float32) * attended.astype(jnp.float32), axis=-1, keepdims=True)
    weight_gradient = jnp.einsum('rft,rwt->rfw', incoming_cotangent_block.astype(jnp.float32), neighbour_values.astype(jnp.float32))
    dscores = probs * (weight_gradient - delta)
    bias_part = jnp.sum(dscores, axis=(0, 1))
    scaled_score_gradient = (dscores * score_scale).astype(jnp.bfloat16)
    query_gradient = jnp.einsum('xtl,xls->xts', scaled_score_gradient.astype(jnp.float32), neighbour_keys.astype(jnp.float32)).astype(jnp.bfloat16)
    key_gradient = jnp.einsum('lyc,lyf->lcf', scaled_score_gradient.astype(jnp.float32), query_block.astype(jnp.float32))
    value_gradient = jnp.einsum('lyc,lyf->lcf', attention_weights.astype(jnp.float32), incoming_cotangent_block.astype(jnp.float32))
    return attended, query_gradient, jnp.concatenate([key_gradient, value_gradient], axis=-1), bias_part


def reference(queries, cotangent, owner, row, table, lengths, bias):
    keys_all = NEIGH * NBR_LEN
    group_rows = N_POOL * NB_DEV
    query_groups = queries.reshape(N_DP, N_POOL, CH_DEV, SPAN, HD)
    cot_groups = cotangent.reshape(N_DP, N_POOL, CH_DEV, SPAN, HD)
    owner_groups = owner.reshape(N_DP, N_POOL, CH_DEV).astype(jnp.int32)
    row_groups = row.reshape(N_DP, N_POOL, CH_DEV).astype(jnp.int32)
    table_groups = table.reshape(N_DP, group_rows, keys_all, 2 * HD)
    length_groups = lengths.reshape(N_DP, group_rows, NEIGH)
    row_bias_values = bias.reshape(keys_all)

    def one_group(operands):
        query_g, cot_g, owner_g, row_g, table_g, length_g = operands

        def one_device(carry, pieces):
            grad_acc, bias_acc = carry
            query_d, cot_d, owner_d, row_d = pieces
            index = (owner_d * NB_DEV + row_d).astype(jnp.int32)
            attended, query_gradient, kv_grad, bias_part = span_pass(query_d, cot_d, table_g[index], length_g[index], row_bias_values)
            grad_acc = grad_acc.at[index].add(kv_grad)
            return (grad_acc, bias_acc + bias_part), (attended, query_gradient)

        start = (jnp.zeros((group_rows, keys_all, 2 * HD), jnp.float32), jnp.zeros((keys_all,), jnp.float32))
        (grad_acc, bias_acc), (attended, query_gradient) = lax.scan(one_device, start, (query_g, cot_g, owner_g, row_g))
        return attended, query_gradient, grad_acc.astype(jnp.bfloat16), bias_acc

    attended, query_gradient, table_grad, bias_parts = lax.map(one_group, (query_groups, cot_groups, owner_groups, row_groups, table_groups, length_groups))
    bias_grad = jnp.sum(bias_parts, axis=0).reshape(HEADS, keys_all)
    return (attended.reshape(TOKENS, HEADS * HD), query_gradient.reshape(TOKENS, HEADS * HD),
            table_grad.reshape(SETS, keys_all, 2 * HD), bias_grad)
```

```python
import functools

import jax
import jax.numpy as jnp
from jax import lax
from jax.experimental import pallas as pl
from jax.experimental.pallas import tpu as pltpu
from jax.sharding import PartitionSpec as P

MESH = pl.DeviceIdType.MESH
NEIGH = 2
CAP = 2
GROUP = 7
NX = 4


def kernel(
    ndp, npool, nx, ny,
    idx_ref, slot_ref, lens_ref, meta_ref, q_ref, c_ref, table_ref, bias_ref,
    att_ref, dq_ref, grad_ref, bgrad_ref,
    meta_got, meta_s, send, recv, back, ret, dsb, wb, rhs, acc, bacc,
    plane, planes,
    meta_ss, meta_rs, meta_cs, send_ss, send_rs, ret_ss, ret_rs,
    b_ss, b_rs, z_ss, z_rs,
):
    dp, me = lax.axis_index("dp"), lax.axis_index("pool")
    core, cx, cy = me % 2, (me // 2) % nx, me // (2 * nx)
    nspans, span, width = q_ref.shape
    nsets, keys, _ = table_ref.shape
    scale = width ** -0.5

    def offsets(s):
        r = s // 2
        b, a = r % ny, r // ny
        return s % 2, (b + a) % nx, (3 * b) % ny

    def place(c, x, y):
        return (y * nx + x) * 2 + c

    def target(s):
        dc, dx, dy = offsets(s)
        return place((core + dc) % 2, (cx + dx) % nx, (cy + dy) % ny)

    def origin(s):
        dc, dx, dy = offsets(s)
        return place((core + 2 - dc) % 2, (cx + nx - dx) % nx, (cy + ny - dy) % ny)

    def remote(src, dst, ss, rs, where):
        return pltpu.make_async_remote_copy(
            src_ref=src, dst_ref=dst, send_sem=ss, recv_sem=rs,
            device_id=where, device_id_type=MESH,
        )

    def each(lo, hi, f):
        def step(i, carry):
            f(i)
            return carry
        lax.fori_loop(lo, hi, step, 0)

    def added(ref, count):
        return lax.fori_loop(0, count, lambda i, total: total + ref[i], jnp.zeros((8, keys), jnp.float32))

    barrier = pltpu.get_barrier_semaphore()
    each(1, npool, lambda s: pl.semaphore_signal(
        barrier, inc=1, device_id={"pool": target(s)}, device_id_type=MESH))
    each(1, ndp, lambda s: pl.semaphore_signal(
        barrier, inc=1, device_id={"dp": (dp + s) % ndp}, device_id_type=MESH))
    pl.semaphore_wait(barrier, npool - 1 + ndp - 1)

    def meta_copy(peer, mine):
        return remote(meta_ref.at[peer], meta_got.at[mine], meta_ss.at[peer], meta_rs.at[mine], {"pool": peer})

    each(1, npool, lambda s: meta_copy(target(s), me).start())
    meta_got[me] = meta_ref[me]

    def pack(peer, buf):
        for k in range(CAP):
            i = idx_ref[peer * CAP + k]
            buf[peer, k, 0] = q_ref[i]
            buf[peer, k, 1] = c_ref[i]

    def data_copy(peer, mine):
        return remote(send.at[peer], recv.at[mine], send_ss.at[peer], send_rs.at[mine], {"pool": peer})

    def ret_copy(peer, mine):
        return remote(back.at[peer], ret.at[mine], ret_ss.at[peer], ret_rs.at[mine], {"pool": peer})

    def out(s):
        peer = target(s)
        pack(peer, send)
        data_copy(peer, me).start()

    each(1, npool, out)
    pack(me, recv)

    acc[...] = jnp.zeros_like(acc)
    bacc[...] = jnp.zeros_like(bacc)
    each(1, npool, lambda s: meta_copy(origin(s), origin(s)).wait_recv())
    to_scalar = pltpu.make_async_copy(meta_got, meta_s, meta_cs)
    to_scalar.start()
    to_scalar.wait()

    def attend(src, at, dest):
        total = jnp.zeros((8, keys), jnp.float32)
        slots = lax.broadcasted_iota(jnp.int32, (1, keys), 1)
        part = keys // NEIGH
        first, position, bias_rows = slots < part, slots % part, bias_ref[...]
        for k in range(CAP):
            row = meta_s[src, 0, k]
            used = row >= 0
            pick = jnp.maximum(row, 0)
            q, c = recv[src, k, 0], recv[src, k, 1]
            kv = table_ref[pick]
            kk, vv = kv[:, :width], kv[:, width:]
            scores = lax.dot_general(q, kk, (((1,), (1,)), ((), ())), preferred_element_type=jnp.float32)
            limit = jnp.where(first, lens_ref[pick * NEIGH], lens_ref[pick * NEIGH + 1])
            extra = jnp.where(position < limit, bias_rows, -1e30)
            scores = scores * scale + extra
            peak = jnp.max(scores, axis=1, keepdims=True)
            e = jnp.exp(scores - peak)
            probs = e / jnp.sum(e, axis=1, keepdims=True)
            weights = probs.astype(jnp.bfloat16)
            att = jnp.dot(weights, vv, preferred_element_type=jnp.float32).astype(jnp.bfloat16)
            delta = jnp.sum(c.astype(jnp.float32) * att.astype(jnp.float32), axis=1, keepdims=True)
            dw = lax.dot_general(c, vv, (((1,), (1,)), ((), ())), preferred_element_type=jnp.float32)
            ds = probs * (dw - delta)
            total = total + jnp.where(used, jnp.sum(ds.reshape(span // 8, 8, keys), axis=0), 0.0)
            dss = (ds * scale).astype(jnp.bfloat16)
            dest[src, k, 0] = att
            dest[src, k, 1] = jnp.dot(dss, kk, preferred_element_type=jnp.float32).astype(jnp.bfloat16)
            rows = pl.ds(pl.multiple_of((at * CAP + k) * span, span), span)
            dsb[rows, :] = dss
            wb[rows, :] = weights
        bacc[...] += total

    def gradients(source, count):
        size = count * CAP * span
        turned = (dsb[pl.ds(0, size), :].T, wb[pl.ds(0, size), :].T)
        for j in range(nsets // 2):
            for which in range(2):
                def fill(t, which=which, j=j):
                    src = source(t)
                    for k in range(CAP):
                        row = meta_s[src, 0, k]
                        x = recv[src, k, which]
                        rows = pl.ds(pl.multiple_of((t * CAP + k) * span, span), span)
                        rhs[rows, :width] = jnp.where(row == 2 * j, x, jnp.zeros_like(x))
                        rhs[rows, width:] = jnp.where(row == 2 * j + 1, x, jnp.zeros_like(x))
                each(0, count, fill)
                acc[j, which] += jnp.dot(turned[which], rhs[pl.ds(0, size), :], preferred_element_type=jnp.float32)

    attend(me, 0, ret)
    gradients(lambda t: me, 1)

    def batch(i):
        def one(t):
            src = origin(1 + i * GROUP + t)
            data_copy(src, src).wait_recv()
            attend(src, t, back)
            ret_copy(src, me).start()
        each(0, GROUP, one)
        gradients(lambda t: origin(1 + i * GROUP + t), GROUP)

    each(0, (npool - 1) // GROUP, batch)

    plane[me] = bacc[...]

    def plane_copy(peer, mine):
        return remote(bacc, plane.at[mine], b_ss.at[peer], b_rs.at[mine], {"pool": peer})

    each(1, npool, lambda s: plane_copy(target(s), me).start())

    for j in range(nsets // 2):
        for which in range(2):
            for h in range(2):
                grad_ref[2 * j + h, :, which * width:(which + 1) * width] = (
                    acc[j, which, :, h * width:(h + 1) * width].astype(jnp.bfloat16))

    each(1, npool, lambda s: plane_copy(origin(s), origin(s)).wait_recv())
    planes[dp] = added(plane, npool)

    def z_copy(peer, mine):
        return remote(planes.at[dp], planes.at[mine], z_ss.at[peer], z_rs.at[mine], {"dp": peer})

    each(1, ndp, lambda s: z_copy((dp + s) % ndp, dp).start())
    each(1, ndp, lambda s: z_copy((dp + s) % ndp, (dp + s) % ndp).wait_recv())
    bgrad_ref[...] = jnp.sum(added(planes, ndp), axis=0, keepdims=True)

    each(1, npool, lambda s: ret_copy(target(s), target(s)).wait_recv())

    def place_out(i):
        slot = slot_ref[i]
        o, k = slot // CAP, slot % CAP
        att_ref[i] = ret[o, k, 0]
        dq_ref[i] = ret[o, k, 1]

    each(0, nspans, place_out)

    def drain(s):
        peer = target(s)
        meta_copy(peer, me).wait_send()
        data_copy(peer, me).wait_send()
        ret_copy(peer, me).wait_send()
        plane_copy(peer, me).wait_send()

    each(1, npool, drain)
    each(1, ndp, lambda s: z_copy((dp + s) % ndp, dp).wait_send())


def body(ndp, npool, nx, ny, queries, cotangent, owner, row, table, lengths, bias):
    nspans = owner.shape[0]
    width = queries.shape[1]
    span = queries.shape[0] // nspans
    nsets, keys, _ = table.shape
    own = owner[:, 0]
    order = jnp.arange(nspans, dtype=jnp.int32)
    rank = jnp.sum(((own[:, None] == own[None, :]) & (order[None, :] < order[:, None])).astype(jnp.int32), axis=1)
    slot = own * CAP + rank
    slots = jnp.arange(npool * CAP, dtype=jnp.int32)
    hit = (slot[None, :] == slots[:, None]).astype(jnp.int32)
    idx = jnp.sum(hit * order[None, :], axis=1)
    sets = jnp.sum(hit * (row + 1)[None, :], axis=1) - 1
    meta = jnp.pad(sets.reshape(npool, 1, CAP), ((0, 0), (0, 0), (0, 128 - CAP)))
    bf, f32 = jnp.bfloat16, jnp.float32
    vmem = pl.BlockSpec(memory_space=pltpu.VMEM)
    smem = pl.BlockSpec(memory_space=pltpu.SMEM)
    dma = pltpu.SemaphoreType.DMA
    rows = GROUP * CAP * span
    att, dq, grad, bgrad = pl.pallas_call(
        functools.partial(kernel, ndp, npool, nx, ny),
        out_shape=(
            jax.ShapeDtypeStruct((nspans, span, width), bf),
            jax.ShapeDtypeStruct((nspans, span, width), bf),
            jax.ShapeDtypeStruct(table.shape, bf),
            jax.ShapeDtypeStruct((1, keys), f32),
        ),
        in_specs=[smem, smem, smem, vmem, vmem, vmem, vmem, vmem],
        out_specs=(vmem, vmem, vmem, vmem),
        scratch_shapes=[
            pltpu.VMEM((npool, 1, 128), jnp.int32),
            pltpu.SMEM((npool, 1, 128), jnp.int32),
            pltpu.VMEM((npool, CAP, 2, span, width), bf),
            pltpu.VMEM((npool, CAP, 2, span, width), bf),
            pltpu.VMEM((npool, CAP, 2, span, width), bf),
            pltpu.VMEM((npool, CAP, 2, span, width), bf),
            pltpu.VMEM((rows, keys), bf),
            pltpu.VMEM((rows, keys), bf),
            pltpu.VMEM((rows, 2 * width), bf),
            pltpu.VMEM((nsets // 2, 2, keys, 2 * width), f32),
            pltpu.VMEM((8, keys), f32),
            pltpu.VMEM((npool, 8, keys), f32),
            pltpu.VMEM((ndp, 8, keys), f32),
            dma((npool,)), dma((npool,)), dma(()),
            dma((npool,)), dma((npool,)),
            dma((npool,)), dma((npool,)),
            dma((npool,)), dma((npool,)),
            dma((ndp,)), dma((ndp,)),
        ],
        compiler_params=pltpu.CompilerParams(
            collective_id=0, has_side_effects=True, vmem_limit_bytes=56 * 1024 * 1024),
    )(
        idx, slot, lengths.reshape(-1), meta,
        queries.reshape(nspans, span, width), cotangent.reshape(nspans, span, width),
        table, bias,
    )
    return att.reshape(queries.shape), dq.reshape(queries.shape), grad, bgrad


def solution(mesh):
    ndp, npool = mesh.shape["dp"], mesh.shape["pool"]
    nx = NX
    ny = npool // (2 * nx)
    pool = P(("dp", "pool"), None)
    cube = P(("dp", "pool"), None, None)
    return jax.shard_map(
        functools.partial(body, ndp, npool, nx, ny),
        mesh=mesh,
        in_specs=(pool, pool, pool, P(("dp", "pool")), cube, pool, P()),
        out_specs=(pool, pool, cube, P()),
        check_vma=False,
    )
```

```python
import functools

import jax
import jax.numpy as jnp
from jax import lax
from jax.experimental import pallas as pl
from jax.experimental.pallas import tpu as pltpu
from jax.sharding import PartitionSpec as P

MESH = pl.DeviceIdType.MESH
NEIGH = 2
CAP = 2
LEAN = 2
GROUP = 7
NX = 4


def lean_kernel(
    ndp, npool, nx, ny,
    lens_ref, own_ref, row_ref, q_ref, c_ref, table_ref, bias_ref,
    att_ref, dq_ref, grad_ref, bgrad_ref, over_ref,
    plan_v, plan_s, mine_v, above_v, above_s, aside_v, meta_v, meta_s,
    send, recv, back, ret, osend, orecv, oback, rsend, rret,
    dsb, wb, rhs, acc, bacc, rowsum, colsum, zsum,
    copy_sem, m_ss, m_rs, n_ss, n_rs, send_ss, send_rs, ret_ss, ret_rs,
    o_ss, o_rs, r_ss, r_rs, rb_ss, rb_rs, ob_ss, ob_rs,
    br_ss, br_rs, bc_ss, bc_rs, z_ss, z_rs,
):
    dp, me = lax.axis_index("dp"), lax.axis_index("pool")
    nrow = 2 * nx
    core, cx, cy, spot = me % 2, (me // 2) % nx, me // nrow, me % nrow
    nspans, span, width = q_ref.shape
    nsets, keys, _ = table_ref.shape
    part = keys // NEIGH
    scale = width ** -0.5

    def offsets(s):
        r = s // 2
        b, a = r % ny, r // ny
        return s % 2, (b + a) % nx, (3 * b) % ny

    def place(c, x, y):
        return (y * nx + x) * 2 + c

    def target(s):
        dc, dx, dy = offsets(s)
        return place((core + dc) % 2, (cx + dx) % nx, (cy + dy) % ny)

    def origin(s):
        dc, dx, dy = offsets(s)
        return place((core + 2 - dc) % 2, (cx + nx - dx) % nx, (cy + ny - dy) % ny)

    def beside(s):
        return ((cx + s // 2) % nx) * 2 + (core + s) % 2

    def above(s):
        return (cy + 3 * s) % ny

    def in_row(m):
        return cy * nrow + m

    def in_column(y):
        return y * nrow + spot

    def remote(src, dst, ss, rs, where):
        return pltpu.make_async_remote_copy(
            src_ref=src, dst_ref=dst, send_sem=ss, recv_sem=rs,
            device_id=where, device_id_type=MESH,
        )

    def each(lo, hi, f):
        def step(i, carry):
            f(i)
            return carry
        lax.fori_loop(lo, hi, step, 0)

    def ask_copy(y, mine):
        return remote(mine_v.at[y], above_v.at[mine], m_ss.at[y], m_rs.at[mine], {"pool": in_column(y)})

    def tell_copy(m, mine):
        return remote(aside_v.at[m], meta_v.at[mine], n_ss.at[m], n_rs.at[mine], {"pool": in_row(m)})

    def data_copy(peer, mine):
        return remote(send.at[peer], recv.at[mine], send_ss.at[peer], send_rs.at[mine], {"pool": peer})

    def ret_copy(peer, mine):
        return remote(back.at[peer], ret.at[mine], ret_ss.at[peer], ret_rs.at[mine], {"pool": peer})

    def over_copy(y, mine):
        return remote(osend.at[y], orecv.at[mine], o_ss.at[y], o_rs.at[mine], {"pool": in_column(y)})

    def row_copy(m, mine):
        return remote(rsend.at[m], recv.at[pl.ds(npool + mine * ny, ny)], r_ss.at[m], r_rs.at[mine], {"pool": in_row(m)})

    def row_back(m, mine):
        return remote(back.at[pl.ds(npool + m * ny, ny)], rret.at[mine], rb_ss.at[m], rb_rs.at[mine], {"pool": in_row(m)})

    def over_back(y, mine):
        return remote(oback.at[y], ret.at[pl.ds(npool + mine * LEAN, LEAN)], ob_ss.at[y], ob_rs.at[mine],
                      {"pool": in_column(y)})

    def row_sum(m, mine):
        return remote(bacc, rowsum.at[mine], br_ss.at[m], br_rs.at[mine], {"pool": in_row(m)})

    def col_sum(y, mine):
        return remote(colsum.at[cy], colsum.at[mine], bc_ss.at[y], bc_rs.at[mine], {"pool": in_column(y)})

    def z_sum(z, mine):
        return remote(zsum.at[dp], zsum.at[mine], z_ss.at[z], z_rs.at[mine], {"dp": z})

    def local(src, dst, k):
        copy = pltpu.make_async_copy(src, dst, copy_sem.at[k])
        copy.start()
        copy.wait()

    barrier = pltpu.get_barrier_semaphore()
    each(1, npool, lambda s: pl.semaphore_signal(
        barrier, inc=1, device_id={"pool": target(s)}, device_id_type=MESH))
    each(1, ndp, lambda s: pl.semaphore_signal(
        barrier, inc=1, device_id={"dp": (dp + s) % ndp}, device_id_type=MESH))

    def plan():
        bits, n = nrow.bit_length() - 1, nspans
        one, many = (lambda x: jnp.where(x, 1, 0)), (lambda x, axis: jnp.sum(x, axis=axis, keepdims=True))
        order_s, order_l = (lax.broadcasted_iota(jnp.int32, shape, axis) for shape, axis in (((n, 1), 0), ((1, n), 1)))
        lanes = lax.broadcasted_iota(jnp.int32, (1, 128), 1)
        peers = lax.broadcasted_iota(jnp.int32, (npool, 1), 0)
        own_s, row_l = own_ref[...], row_ref[...]
        own_l = many(one(order_s == order_l) * own_s, 0)
        same = one(own_s == own_l)
        rank_s, rank_l = many(same * one(order_l < order_s), 1), many(same * one(order_s < order_l), 0)
        home_s, home_l, local_l = own_s >> bits, own_l >> bits, own_l & (nrow - 1)
        near = one(home_s == home_l)
        place_s = many(near * one(own_l < own_s) * rank_l, 1)
        place_l = many(near * one(own_s < own_l) * rank_s, 0)
        carried_s, carried_l = rank_s * one(place_s < LEAN), rank_l * one(place_l < LEAN)
        slot_s = rank_s * (npool + home_s * LEAN + jnp.minimum(place_s, LEAN - 1)) + (1 - rank_s) * own_s
        taken_s = (1 - rank_s) + carried_s
        plan_v[0:1, :] = many(one(slot_s == lanes) * (taken_s * order_s), 0)
        plan_v[1:2, :] = many(one(order_s == lanes) * slot_s, 0)
        at_peer, at_row = one(own_l == peers), one(home_l == (peers >> bits))
        fields = [
            many(at_peer * ((1 - rank_l) * (row_l + 1)), 1) - 1,
            many(at_peer * (carried_l * (row_l + 1)), 1) - 1,
            many(at_peer * (carried_l * place_l), 1),
        ] + [many(at_row * (carried_l * one(place_l == j) * local_l), 1) for j in range(LEAN)]
        meta = jnp.zeros((npool, 128), jnp.int32)
        for k, field in enumerate(fields):
            meta = jnp.where(lanes == k, field, meta)
        mine_v[...] = meta.reshape(ny, nrow, 128)
        over = many(rank_l * one(place_l >= LEAN), 1).astype(jnp.float32)
        bacc[:, :keys] = jnp.zeros((8, keys), jnp.float32)
        bacc[:, keys:] = jnp.broadcast_to(over, (8, 128))
        local(plan_v, plan_s, 0)

    def pack_over(y, buf):
        for j in range(LEAN):
            i = jnp.clip(plan_s[0, npool + y * LEAN + j], 0, nspans - 1)
            buf[y, j, 0] = q_ref[i]
            buf[y, j, 1] = c_ref[i]

    def pack(peer, buf):
        i = jnp.clip(plan_s[0, peer], 0, nspans - 1)
        buf[peer, 0] = q_ref[i]
        buf[peer, 1] = c_ref[i]

    plan()
    each(1, ny, lambda s: pack_over(above(s), osend))
    pack_over(cy, orecv)
    above_v[cy] = mine_v[cy]
    pl.semaphore_wait(barrier, npool - 1 + ndp - 1)

    each(1, ny, lambda s: ask_copy(above(s), cy).start())
    each(1, ny, lambda s: over_copy(above(s), cy).start())

    def out(s):
        peer = target(s)
        pack(peer, send)
        data_copy(peer, me).start()

    stride = (2 * npool // 3) // (nrow - 1)
    ahead = npool - stride * (nrow - 1)
    each(1, ahead, out)
    pack(me, recv)

    each(1, ny, lambda s: ask_copy(above(s), above(s)).wait_recv())
    for m in range(nrow):
        for y in range(ny):
            aside_v[m, y:y + 1, :] = above_v[y, m:m + 1, :]
    each(1, nrow, lambda s: tell_copy(beside(s), spot).start())
    meta_v[spot] = aside_v[spot]
    local(above_v, above_s, 1)
    acc[...] = jnp.zeros_like(acc)

    def fill(m, put):
        def one(y):
            j = jnp.clip(above_s[y, m, 2], 0, LEAN - 1)
            put(y, orecv[y, j])
        each(0, ny, one)

    def relay_in(s):
        m = beside(s)
        def put(y, x):
            rsend[m, y] = x
        fill(m, put)
        row_copy(m, spot).start()
        each(ahead + (s - 1) * stride, ahead + s * stride, out)

    each(1, ny, lambda s: over_copy(above(s), above(s)).wait_recv())
    each(1, nrow, relay_in)
    def put(y, x):
        recv[npool + spot * ny + y] = x
    fill(spot, put)
    each(1, nrow, lambda s: tell_copy(beside(s), beside(s)).wait_recv())
    local(meta_v, meta_s, 2)

    def relay_out():
        def keep(y):
            rret[spot, y] = back[npool + spot * ny + y]
        each(0, ny, keep)
        each(1, nrow, lambda s: row_back(beside(s), beside(s)).wait_recv())

        def go(s):
            y = above(s)
            for j in range(LEAN):
                m = jnp.clip(above_s[y, 0, 3 + j], 0, nrow - 1)
                oback[y, j] = rret[m, y]
            over_back(y, cy).start()

        each(1, ny, go)
        for j in range(LEAN):
            m = jnp.clip(above_s[cy, 0, 3 + j], 0, nrow - 1)
            ret[npool + cy * LEAN + j] = rret[m, cy]

    def attend(items):
        count = len(items)
        slots = lax.broadcasted_iota(jnp.int32, (1, keys), 1)
        first, position, bias_rows = slots < part, slots % part, bias_ref[...]
        blank = jnp.zeros((span, width), jnp.bfloat16)
        kvs, both = [], []
        for source, row, dest in items:
            q, c = source[0], source[1]
            kv = table_ref[jnp.clip(row, 0, nsets - 1)]
            wide = jnp.concatenate(
                [jnp.concatenate([q, blank], axis=1), jnp.concatenate([blank, c], axis=1)], axis=0)
            kvs.append(kv)
            both.append(lax.dot_general(wide, kv, (((1,), (1,)), ((), ())), preferred_element_type=jnp.float32))
        total = jnp.zeros((8, keys), jnp.float32)
        probs = []
        for t, (source, row, dest) in enumerate(items):
            pick = jnp.clip(row, 0, nsets - 1)
            limit = jnp.where(first, lens_ref[pick, 0], lens_ref[pick, 1])
            extra = jnp.where(position < limit, bias_rows, -1e30)
            scores = both[t][:span] * scale + extra
            e = jnp.exp(scores - jnp.max(scores, axis=1, keepdims=True))
            probs.append(e * (1.0 / jnp.sum(e, axis=1, keepdims=True)))
            wb[t * span:(t + 1) * span, :] = probs[t].astype(jnp.bfloat16)
        deltas = []
        for t, (source, row, dest) in enumerate(items):
            att = jnp.dot(probs[t].astype(jnp.bfloat16), kvs[t][:, width:], preferred_element_type=jnp.float32)
            att = att.astype(jnp.bfloat16)
            dest[0] = att
            deltas.append(jnp.sum(source[1].astype(jnp.float32) * att.astype(jnp.float32), axis=1, keepdims=True))
        for t, (source, row, dest) in enumerate(items):
            ds = probs[t] * (both[t][span:] - deltas[t])
            total = total + jnp.where(row >= 0, jnp.sum(ds.reshape(span // 8, 8, keys), axis=0), 0.0)
            dss = (ds * scale).astype(jnp.bfloat16)
            dsb[t * span:(t + 1) * span, :] = dss
            dest[1] = jnp.dot(dss, kvs[t][:, :width], preferred_element_type=jnp.float32).astype(jnp.bfloat16)
        bacc[:, :keys] += total
        size = count * span
        for which, left in ((0, dsb), (1, wb)):
            for t, (source, row, dest) in enumerate(items):
                x = source[which]
                for n in range(nsets):
                    rhs[which, t * span:(t + 1) * span, n * width:(n + 1) * width] = jnp.where(row == n, x, blank)
            acc[which] += lax.dot_general(
                left[:size, :], rhs[which, :size, :], (((0,), (0,)), ((), ())), preferred_element_type=jnp.float32)

    cut, last = 3 * nrow // 2, 2 * nrow

    def batch(k):
        late = k // cut
        second = (1 - late) * ((k % 3 + 1) // 2)
        b = (1 - late) * (k // 3) + late * (k - nrow)
        m = beside((1 - late) * second * (2 * (k // 3) + k % 3 - 1))

        @pl.when(k == last - 2)
        def _():
            relay_out()

        def wait_first(t):
            src = origin(b * ny + t)

            @pl.when((1 - second) * (b * ny + t) > 0)
            def _():
                data_copy(src, src).wait_recv()

        each(0, ny, wait_first)
        aside = (spot + nrow - m) % nrow

        @pl.when(second * aside > 0)
        def _():
            row_copy(m, m).wait_recv()

        items = []
        for t in range(ny):
            src = origin(b * ny + t)
            at = (1 - second) * src + second * (npool + m * ny + t)
            row = meta_s[(1 - second) * (src % nrow) + second * m, (1 - second) * (src // nrow) + second * t, second]
            items.append((recv.at[at], row, back.at[at]))
        attend(items)

        def send_first(t):
            src = origin(b * ny + t)

            @pl.when((1 - second) * (b * ny + t) > 0)
            def _():
                ret_copy(src, me).start()

        each(0, ny, send_first)

        @pl.when(second * aside > 0)
        def _():
            row_back(m, spot).start()

    each(0, last, batch)
    ret[me] = back[me]

    def added(ref, count):
        return lax.fori_loop(0, count, lambda i, total: total + ref[i], jnp.zeros(bacc.shape, jnp.float32))

    rowsum[spot] = bacc[...]
    each(1, nrow, lambda s: row_sum(beside(s), spot).start())
    for which in range(2):
        for n in range(nsets):
            grad_ref[n, :, which * width:(which + 1) * width] = (
                acc[which, :, n * width:(n + 1) * width].astype(jnp.bfloat16))
    each(1, nrow, lambda s: row_sum(beside(s), beside(s)).wait_recv())
    colsum[cy] = added(rowsum, nrow)
    each(1, ny, lambda s: col_sum(above(s), cy).start())
    each(1, ny, lambda s: col_sum(above(s), above(s)).wait_recv())
    zsum[dp] = added(colsum, ny)
    each(1, ndp, lambda s: z_sum((dp + s) % ndp, dp).start())
    each(1, ndp, lambda s: z_sum((dp + s) % ndp, (dp + s) % ndp).wait_recv())
    whole = added(zsum, ndp)
    bgrad_ref[...] = jnp.sum(whole[:, :keys], axis=0, keepdims=True)
    over_ref[...] = whole[:, keys:]

    each(1, npool, lambda s: ret_copy(target(s), target(s)).wait_recv())
    each(1, ny, lambda s: over_back(above(s), above(s)).wait_recv())

    def place_out(i):
        slot = jnp.clip(plan_s[1, i], 0, npool + ny * LEAN - 1)
        att_ref[i] = ret[slot, 0]
        dq_ref[i] = ret[slot, 1]

    each(0, nspans, place_out)

    def drain(s):
        peer = target(s)
        data_copy(peer, me).wait_send()
        ret_copy(peer, me).wait_send()

    each(1, npool, drain)
    each(1, ny, lambda s: ask_copy(above(s), cy).wait_send())
    each(1, nrow, lambda s: tell_copy(beside(s), spot).wait_send())
    each(1, nrow, lambda s: row_sum(beside(s), spot).wait_send())
    each(1, ny, lambda s: col_sum(above(s), cy).wait_send())
    each(1, ny, lambda s: over_copy(above(s), cy).wait_send())
    each(1, ny, lambda s: over_back(above(s), cy).wait_send())
    each(1, nrow, lambda s: row_copy(beside(s), spot).wait_send())
    each(1, nrow, lambda s: row_back(beside(s), spot).wait_send())
    each(1, ndp, lambda s: z_sum((dp + s) % ndp, dp).wait_send())


def wide_kernel(
    ndp, npool, nx, ny,
    idx_ref, slot_ref, lens_ref, meta_ref, q_ref, c_ref, table_ref, bias_ref,
    att_ref, dq_ref, grad_ref, bgrad_ref,
    meta_got, meta_s, send, recv, back, ret, dsb, wb, rhs, acc, bacc,
    plane, planes,
    meta_ss, meta_rs, meta_cs, send_ss, send_rs, ret_ss, ret_rs,
    b_ss, b_rs, z_ss, z_rs,
):
    dp, me = lax.axis_index("dp"), lax.axis_index("pool")
    core, cx, cy = me % 2, (me // 2) % nx, me // (2 * nx)
    nspans, span, width = q_ref.shape
    nsets, keys, _ = table_ref.shape
    scale = width ** -0.5

    def offsets(s):
        r = s // 2
        b, a = r % ny, r // ny
        return s % 2, (b + a) % nx, (3 * b) % ny

    def place(c, x, y):
        return (y * nx + x) * 2 + c

    def target(s):
        dc, dx, dy = offsets(s)
        return place((core + dc) % 2, (cx + dx) % nx, (cy + dy) % ny)

    def origin(s):
        dc, dx, dy = offsets(s)
        return place((core + 2 - dc) % 2, (cx + nx - dx) % nx, (cy + ny - dy) % ny)

    def remote(src, dst, ss, rs, where):
        return pltpu.make_async_remote_copy(
            src_ref=src, dst_ref=dst, send_sem=ss, recv_sem=rs,
            device_id=where, device_id_type=MESH,
        )

    def each(lo, hi, f):
        def step(i, carry):
            f(i)
            return carry
        lax.fori_loop(lo, hi, step, 0)

    def added(ref, count):
        return lax.fori_loop(0, count, lambda i, total: total + ref[i], jnp.zeros((8, keys), jnp.float32))

    barrier = pltpu.get_barrier_semaphore()
    each(1, npool, lambda s: pl.semaphore_signal(
        barrier, inc=1, device_id={"pool": target(s)}, device_id_type=MESH))
    each(1, ndp, lambda s: pl.semaphore_signal(
        barrier, inc=1, device_id={"dp": (dp + s) % ndp}, device_id_type=MESH))
    pl.semaphore_wait(barrier, npool - 1 + ndp - 1)

    def meta_copy(peer, mine):
        return remote(meta_ref.at[peer], meta_got.at[mine], meta_ss.at[peer], meta_rs.at[mine], {"pool": peer})

    each(1, npool, lambda s: meta_copy(target(s), me).start())
    meta_got[me] = meta_ref[me]

    def pack(peer, buf):
        for k in range(CAP):
            i = idx_ref[peer * CAP + k]
            buf[peer, k, 0] = q_ref[i]
            buf[peer, k, 1] = c_ref[i]

    def data_copy(peer, mine):
        return remote(send.at[peer], recv.at[mine], send_ss.at[peer], send_rs.at[mine], {"pool": peer})

    def ret_copy(peer, mine):
        return remote(back.at[peer], ret.at[mine], ret_ss.at[peer], ret_rs.at[mine], {"pool": peer})

    def out(s):
        peer = target(s)
        pack(peer, send)
        data_copy(peer, me).start()

    each(1, npool, out)
    pack(me, recv)

    acc[...] = jnp.zeros_like(acc)
    bacc[...] = jnp.zeros_like(bacc)
    each(1, npool, lambda s: meta_copy(origin(s), origin(s)).wait_recv())
    to_scalar = pltpu.make_async_copy(meta_got, meta_s, meta_cs)
    to_scalar.start()
    to_scalar.wait()

    def attend(src, at, dest):
        total = jnp.zeros((8, keys), jnp.float32)
        slots = lax.broadcasted_iota(jnp.int32, (1, keys), 1)
        part = keys // NEIGH
        first, position, bias_rows = slots < part, slots % part, bias_ref[...]
        for k in range(CAP):
            row = meta_s[src, 0, k]
            used = row >= 0
            pick = jnp.maximum(row, 0)
            q, c = recv[src, k, 0], recv[src, k, 1]
            kv = table_ref[pick]
            kk, vv = kv[:, :width], kv[:, width:]
            scores = lax.dot_general(q, kk, (((1,), (1,)), ((), ())), preferred_element_type=jnp.float32)
            limit = jnp.where(first, lens_ref[pick * NEIGH], lens_ref[pick * NEIGH + 1])
            extra = jnp.where(position < limit, bias_rows, -1e30)
            scores = scores * scale + extra
            peak = jnp.max(scores, axis=1, keepdims=True)
            e = jnp.exp(scores - peak)
            probs = e / jnp.sum(e, axis=1, keepdims=True)
            weights = probs.astype(jnp.bfloat16)
            att = jnp.dot(weights, vv, preferred_element_type=jnp.float32).astype(jnp.bfloat16)
            delta = jnp.sum(c.astype(jnp.float32) * att.astype(jnp.float32), axis=1, keepdims=True)
            dw = lax.dot_general(c, vv, (((1,), (1,)), ((), ())), preferred_element_type=jnp.float32)
            ds = probs * (dw - delta)
            total = total + jnp.where(used, jnp.sum(ds.reshape(span // 8, 8, keys), axis=0), 0.0)
            dss = (ds * scale).astype(jnp.bfloat16)
            dest[src, k, 0] = att
            dest[src, k, 1] = jnp.dot(dss, kk, preferred_element_type=jnp.float32).astype(jnp.bfloat16)
            rows = pl.ds(pl.multiple_of((at * CAP + k) * span, span), span)
            dsb[rows, :] = dss
            wb[rows, :] = weights
        bacc[...] += total

    def gradients(source, count):
        size = count * CAP * span
        turned = (dsb[pl.ds(0, size), :].T, wb[pl.ds(0, size), :].T)
        for j in range(nsets // 2):
            for which in range(2):
                def fill(t, which=which, j=j):
                    src = source(t)
                    for k in range(CAP):
                        row = meta_s[src, 0, k]
                        x = recv[src, k, which]
                        rows = pl.ds(pl.multiple_of((t * CAP + k) * span, span), span)
                        rhs[rows, :width] = jnp.where(row == 2 * j, x, jnp.zeros_like(x))
                        rhs[rows, width:] = jnp.where(row == 2 * j + 1, x, jnp.zeros_like(x))
                each(0, count, fill)
                acc[j, which] += jnp.dot(turned[which], rhs[pl.ds(0, size), :], preferred_element_type=jnp.float32)

    attend(me, 0, ret)
    gradients(lambda t: me, 1)

    def batch(i):
        def one(t):
            src = origin(1 + i * GROUP + t)
            data_copy(src, src).wait_recv()
            attend(src, t, back)
            ret_copy(src, me).start()
        each(0, GROUP, one)
        gradients(lambda t: origin(1 + i * GROUP + t), GROUP)

    each(0, (npool - 1) // GROUP, batch)

    plane[me] = bacc[...]

    def plane_copy(peer, mine):
        return remote(bacc, plane.at[mine], b_ss.at[peer], b_rs.at[mine], {"pool": peer})

    each(1, npool, lambda s: plane_copy(target(s), me).start())

    for j in range(nsets // 2):
        for which in range(2):
            for h in range(2):
                grad_ref[2 * j + h, :, which * width:(which + 1) * width] = (
                    acc[j, which, :, h * width:(h + 1) * width].astype(jnp.bfloat16))

    each(1, npool, lambda s: plane_copy(origin(s), origin(s)).wait_recv())
    planes[dp] = added(plane, npool)

    def z_copy(peer, mine):
        return remote(planes.at[dp], planes.at[mine], z_ss.at[peer], z_rs.at[mine], {"dp": peer})

    each(1, ndp, lambda s: z_copy((dp + s) % ndp, dp).start())
    each(1, ndp, lambda s: z_copy((dp + s) % ndp, (dp + s) % ndp).wait_recv())
    bgrad_ref[...] = jnp.sum(added(planes, ndp), axis=0, keepdims=True)

    each(1, npool, lambda s: ret_copy(target(s), target(s)).wait_recv())

    def place_out(i):
        slot = slot_ref[i]
        o, k = slot // CAP, slot % CAP
        att_ref[i] = ret[o, k, 0]
        dq_ref[i] = ret[o, k, 1]

    each(0, nspans, place_out)

    def drain(s):
        peer = target(s)
        meta_copy(peer, me).wait_send()
        data_copy(peer, me).wait_send()
        ret_copy(peer, me).wait_send()
        plane_copy(peer, me).wait_send()

    each(1, npool, drain)
    each(1, ndp, lambda s: z_copy((dp + s) % ndp, dp).wait_send())


def wide(ndp, npool, nx, ny, queries, cotangent, owner, row, table, lengths, bias):
    nspans = owner.shape[0]
    width = queries.shape[1]
    span = queries.shape[0] // nspans
    nsets, keys, _ = table.shape
    own = owner[:, 0]
    order = jnp.arange(nspans, dtype=jnp.int32)
    rank = jnp.sum(((own[:, None] == own[None, :]) & (order[None, :] < order[:, None])).astype(jnp.int32), axis=1)
    slot = own * CAP + rank
    slots = jnp.arange(npool * CAP, dtype=jnp.int32)
    hit = (slot[None, :] == slots[:, None]).astype(jnp.int32)
    idx = jnp.sum(hit * order[None, :], axis=1)
    sets = jnp.sum(hit * (row + 1)[None, :], axis=1) - 1
    meta = jnp.pad(sets.reshape(npool, 1, CAP), ((0, 0), (0, 0), (0, 128 - CAP)))
    bf, f32 = jnp.bfloat16, jnp.float32
    vmem = pl.BlockSpec(memory_space=pltpu.VMEM)
    smem = pl.BlockSpec(memory_space=pltpu.SMEM)
    dma = pltpu.SemaphoreType.DMA
    rows = GROUP * CAP * span
    att, dq, grad, bgrad = pl.pallas_call(
        functools.partial(wide_kernel, ndp, npool, nx, ny),
        out_shape=(
            jax.ShapeDtypeStruct((nspans, span, width), bf),
            jax.ShapeDtypeStruct((nspans, span, width), bf),
            jax.ShapeDtypeStruct(table.shape, bf),
            jax.ShapeDtypeStruct((1, keys), f32),
        ),
        in_specs=[smem, smem, smem, vmem, vmem, vmem, vmem, vmem],
        out_specs=(vmem, vmem, vmem, vmem),
        scratch_shapes=[
            pltpu.VMEM((npool, 1, 128), jnp.int32),
            pltpu.SMEM((npool, 1, 128), jnp.int32),
            pltpu.VMEM((npool, CAP, 2, span, width), bf),
            pltpu.VMEM((npool, CAP, 2, span, width), bf),
            pltpu.VMEM((npool, CAP, 2, span, width), bf),
            pltpu.VMEM((npool, CAP, 2, span, width), bf),
            pltpu.VMEM((rows, keys), bf),
            pltpu.VMEM((rows, keys), bf),
            pltpu.VMEM((rows, 2 * width), bf),
            pltpu.VMEM((nsets // 2, 2, keys, 2 * width), f32),
            pltpu.VMEM((8, keys), f32),
            pltpu.VMEM((npool, 8, keys), f32),
            pltpu.VMEM((ndp, 8, keys), f32),
            dma((npool,)), dma((npool,)), dma(()),
            dma((npool,)), dma((npool,)),
            dma((npool,)), dma((npool,)),
            dma((npool,)), dma((npool,)),
            dma((ndp,)), dma((ndp,)),
        ],
        compiler_params=pltpu.CompilerParams(
            collective_id=1, has_side_effects=True, vmem_limit_bytes=56 * 1024 * 1024),
    )(
        idx, slot, lengths.reshape(-1), meta,
        queries.reshape(nspans, span, width), cotangent.reshape(nspans, span, width),
        table, bias,
    )
    return att.reshape(queries.shape), dq.reshape(queries.shape), grad, bgrad


def lean(ndp, npool, nx, ny, queries, cotangent, owner, row, table, lengths, bias):
    nspans = owner.shape[0]
    width = queries.shape[1]
    span = queries.shape[0] // nspans
    nsets, keys, _ = table.shape
    nrow = 2 * nx
    bf, f32 = jnp.bfloat16, jnp.float32
    vmem = pl.BlockSpec(memory_space=pltpu.VMEM)
    smem = pl.BlockSpec(memory_space=pltpu.SMEM)
    dma = pltpu.SemaphoreType.DMA
    rows = ny * span
    att, dq, grad, bgrad, over = pl.pallas_call(
        functools.partial(lean_kernel, ndp, npool, nx, ny),
        out_shape=(
            jax.ShapeDtypeStruct((nspans, span, width), bf),
            jax.ShapeDtypeStruct((nspans, span, width), bf),
            jax.ShapeDtypeStruct(table.shape, bf),
            jax.ShapeDtypeStruct((1, keys), f32),
            jax.ShapeDtypeStruct((8, 128), f32),
        ),
        in_specs=[smem, vmem, vmem, vmem, vmem, vmem, vmem],
        out_specs=(vmem, vmem, vmem, vmem, vmem),
        scratch_shapes=[
            pltpu.VMEM((8, 128), jnp.int32),
            pltpu.SMEM((8, 128), jnp.int32),
            pltpu.VMEM((ny, nrow, 128), jnp.int32),
            pltpu.VMEM((ny, nrow, 128), jnp.int32),
            pltpu.SMEM((ny, nrow, 128), jnp.int32),
            pltpu.VMEM((nrow, ny, 128), jnp.int32),
            pltpu.VMEM((nrow, ny, 128), jnp.int32),
            pltpu.SMEM((nrow, ny, 128), jnp.int32),
            pltpu.VMEM((npool, 2, span, width), bf),
            pltpu.VMEM((2 * npool, 2, span, width), bf),
            pltpu.VMEM((2 * npool, 2, span, width), bf),
            pltpu.VMEM((npool + ny * LEAN, 2, span, width), bf),
            pltpu.VMEM((ny, LEAN, 2, span, width), bf),
            pltpu.VMEM((ny, LEAN, 2, span, width), bf),
            pltpu.VMEM((ny, LEAN, 2, span, width), bf),
            pltpu.VMEM((nrow, ny, 2, span, width), bf),
            pltpu.VMEM((nrow, ny, 2, span, width), bf),
            pltpu.VMEM((rows, keys), bf),
            pltpu.VMEM((rows, keys), bf),
            pltpu.VMEM((2, rows, nsets * width), bf),
            pltpu.VMEM((2, keys, nsets * width), f32),
            pltpu.VMEM((8, keys + 128), f32),
            pltpu.VMEM((nrow, 8, keys + 128), f32),
            pltpu.VMEM((ny, 8, keys + 128), f32),
            pltpu.VMEM((ndp, 8, keys + 128), f32),
            dma((3,)), dma((ny,)), dma((ny,)), dma((nrow,)), dma((nrow,)),
            dma((npool,)), dma((npool,)),
            dma((npool,)), dma((npool,)),
            dma((ny,)), dma((ny,)), dma((nrow,)), dma((nrow,)),
            dma((nrow,)), dma((nrow,)), dma((ny,)), dma((ny,)),
            dma((nrow,)), dma((nrow,)), dma((ny,)), dma((ny,)), dma((ndp,)), dma((ndp,)),
        ],
        compiler_params=pltpu.CompilerParams(
            collective_id=0, has_side_effects=True, vmem_limit_bytes=56 * 1024 * 1024),
    )(
        lengths, owner, row.reshape(1, nspans),
        queries.reshape(nspans, span, width), cotangent.reshape(nspans, span, width),
        table, bias,
    )
    return (att.reshape(queries.shape), dq.reshape(queries.shape), grad, bgrad), over[0, 0] > 0


def body(ndp, npool, nx, ny, *args):
    outs, short = lean(ndp, npool, nx, ny, *args)
    return lax.cond(short, lambda kept: wide(ndp, npool, nx, ny, *args), lambda kept: kept, outs)


def solution(mesh):
    ndp, npool = mesh.shape["dp"], mesh.shape["pool"]
    nx = NX
    ny = npool // (2 * nx)
    pool = P(("dp", "pool"), None)
    cube = P(("dp", "pool"), None, None)
    return jax.shard_map(
        functools.partial(body, ndp, npool, nx, ny),
        mesh=mesh,
        in_specs=(pool, pool, pool, P(("dp", "pool")), cube, pool, P()),
        out_specs=(pool, pool, cube, P()),
        check_vma=False,
    )
```
